32 devices in a mesh: member: 8 (over y, x, core), space: 4 (over z).
Axes of the slice: x: 2, y: 2, z: 4, core: 2. Of those that a mesh axis runs over, the one named last changes fastest.
Arguments:
- realization_channels: bfloat16 [8, 4096, 1024], P('member', 'space'), may hold values from -6 to 6
- node_gain: bfloat16 [1024], replicated, may hold values from 0.5 to 1.5
- w_self: bfloat16 [1024, 1024], replicated, may hold values from -0.1875 to 0.1875
- w_neighbour: bfloat16 [1024, 1024], replicated, may hold values from -0.1875 to 0.1875
- w_out: bfloat16 [1024, 1024], replicated, may hold values from -0.1875 to 0.1875
- readout_map: bfloat16 [100, 1024], replicated, may hold values from -0.1875 to 0.1875
- edge_index: int32 [4096, 8], P('space'), may hold values from 0 to 1279, as said below
- verifying_truth: float32 [100, 4096], P(None, 'space'), may hold values from -6 to 6
- var_weight: float32 [100], replicated, may hold values from 0.3 to 3
- area_weight: float32 [4096], P('space'), may hold values from 0.3 to 3
Outputs:
- grad_hidden: bfloat16 [8, 4096, 1024], P('member', 'space')
- grad_decoder: float32 [100, 1024], replicated
The draws below stay inside these ranges and needn't reach their ends.
Inputs may be any that keep to these rules, and one draw needn't show every extreme that they name: `edge_index`: entry e of a node at position i of its shard's 1024 nodes lies within 128 of i + 128.
All inputs are finite; a program needn't handle non-finite values.
Results may differ from the reference program's by a relative error of at most 0.012.
The reference program's roundings to bfloat16 on the way count: a program that leaves them out, or rounds other values in their place, can miss the bound.
Values may be sent and summed in bfloat16 or wider, within the bound.
A program may use at most 128 MiB of HBM per device.

```python
import math
import jax
import jax.numpy as jnp
from jax import lax

H = 1024
VARS = 100
K = 8
HALO = 128
NODES_DEV = 1024
NODES = 4096
MEMBERS = 8


def draw_edge_index(key, part):
    key = jax.random.fold_in(key, 5)
    offsets = jax.random.randint(key, (NODES, K), -HALO, HALO + 1)
    position = jnp.arange(NODES) % NODES_DEV
    first = jnp.where(position == 0, -HALO, offsets[:, 0])
    first = jnp.where(position == NODES_DEV - 1, HALO, first)
    offsets = offsets.at[:, 0].set(first)
    return (position[:, None] + HALO + offsets).astype(jnp.int32)


def level_of(key, shape, cuts, smallest, largest):
    factor_of, own = 1.0, jax.random.fold_in(key, 6)
    for dim, shards_of in cuts:
        steps = jnp.exp(jax.random.uniform(jax.random.fold_in(own, dim), (shards_of,), jnp.float32, smallest / len(cuts), largest / len(cuts)))
        factor_of = factor_of * jnp.repeat(steps, shape[dim] // shards_of).reshape([-1 if axis == dim else 1 for axis in range(len(shape))])
    return factor_of


def gaussian(own_key, shape, deviation, reach, cuts=(), held_as=jnp.bfloat16):
    loudness = level_of(own_key, shape, cuts, -0.22, 0.18) if cuts else 1.0
    result = jax.random.normal(own_key, shape, jnp.float32) * deviation * loudness
    return jnp.minimum(jnp.maximum(result, -reach), reach).astype(held_as)


def setup_inputs(seed: int = 0) -> dict:
    key_of = jax.random.split(jax.random.key(seed), 11)
    return {
        "realization_channels": gaussian(key_of[0], (MEMBERS, NODES, H), 1.0, 6.0, ((0, 8), (1, 4))),
        "node_gain": jnp.clip(1.0 + 0.1 * jax.random.normal(key_of[1], (H,), jnp.float32), 0.5, 1.5).astype(jnp.bfloat16),
        "w_self": gaussian(key_of[2], (H, H), H ** -0.5, 0.1875),
        "w_neighbour": gaussian(key_of[3], (H, H), H ** -0.5, 0.1875),
        "w_out": gaussian(key_of[4], (H, H), H ** -0.5, 0.1875),
        "readout_map": gaussian(key_of[5], (VARS, H), H ** -0.5, 0.1875),
        "edge_index": draw_edge_index(jax.random.fold_in(key_of[10], 71), 0),
        "verifying_truth": gaussian(key_of[7], (VARS, NODES), 1.0, 6.0, ((1, 4),), jnp.float32),
        "var_weight": jnp.clip(jnp.exp(jax.random.uniform(key_of[8], (VARS,), jnp.float32, math.log(0.3), math.log(3.0))), 0.3, 3.0),
        "area_weight": jnp.clip(jnp.exp(math.log(3.0) - 2.3025851 * jax.random.uniform(key_of[9], (NODES,), jnp.float32) ** level_of(key_of[9], (NODES,), ((0, 4),), -0.2, 0.2)), 0.3, 3.0),
    }


TAU = 0.05
ALPHA = 0.95

def softened_sign(diff):
    return diff / jnp.sqrt(diff * diff + TAU * TAU)

def reference(realization_channels, node_gain, w_self, w_neighbour, w_out, readout_map, edge_index, verifying_truth, var_weight, area_weight):
    shards = NODES // NODES_DEV
    edges_three = edge_index.reshape(shards, NODES_DEV, K)
    members = realization_channels.shape[0]

    def lone_realization(member_now):
        values = member_now.astype(jnp.float32)
        scale = lax.rsqrt(lax.optimization_barrier(jnp.mean(values * values, axis=-1, keepdims=True)) + 1e-06)
        normed = (values * scale * node_gain.astype(jnp.float32)).astype(jnp.bfloat16)
        blocks = normed.reshape(shards, NODES_DEV, H)
        empty_rows = jnp.zeros((1, HALO, H), jnp.bfloat16)
        lower_rim = jnp.concatenate([empty_rows, blocks[:-1, NODES_DEV - HALO:]], axis=0)
        upper_rim = jnp.concatenate([blocks[1:, :HALO], empty_rows], axis=0)
        extended = jnp.concatenate([lower_rim, blocks, upper_rim], axis=1)
        summed = jnp.zeros((shards, NODES_DEV, H), jnp.float32)
        for column in range(K):
            picked = jax.vmap(lambda block, index: block[index])(extended, edges_three[:, :, column])
            summed = summed + picked.astype(jnp.float32)
        neighbour_mean = (summed / K).astype(jnp.bfloat16).reshape(NODES, H)
        inside = jnp.dot(normed, w_self, preferred_element_type=jnp.float32) + jnp.dot(neighbour_mean, w_neighbour, preferred_element_type=jnp.float32)
        activated = jax.nn.gelu(inside).astype(jnp.bfloat16)
        latent_channels = (values + jnp.dot(activated, w_out, preferred_element_type=jnp.float32)).astype(jnp.bfloat16)
        prediction_field = lax.dot_general(readout_map, latent_channels, (((1,), (1,)), ((), ())), preferred_element_type=jnp.float32)
        return (latent_channels, prediction_field)
    latent_channels, prediction_field = lax.map(lone_realization, realization_channels)
    linear_operator = var_weight[:, None] * area_weight[None, :]
    eps = (1.0 - ALPHA) / members
    couple_factor = (1.0 - eps) / (members - 1)

    def realization_derivative(current_prediction):
        collective_dispersion = lax.optimization_barrier(jnp.sum(softened_sign(current_prediction[None] - prediction_field), axis=0))
        return (linear_operator * (softened_sign(current_prediction - verifying_truth) - couple_factor * collective_dispersion)).astype(jnp.bfloat16)
    couple_derivatives = lax.map(realization_derivative, prediction_field)

    def back_hidden(grad_one):
        return lax.dot_general(grad_one, readout_map, (((0,), (0,)), ((), ())), preferred_element_type=jnp.float32).astype(jnp.bfloat16)
    grad_hidden = lax.map(back_hidden, couple_derivatives)

    def add_term(carry, pair):
        grad_one, hidden_one = pair
        return (carry + jnp.dot(grad_one, hidden_one, preferred_element_type=jnp.float32), None)
    grad_decoder, _ = lax.scan(add_term, jnp.zeros((VARS, H), jnp.float32), (couple_derivatives, latent_channels))
    grad_decoder = grad_decoder / jnp.sqrt(jnp.float32(members * NODES))
    return (grad_hidden, grad_decoder)
```

```python
import functools
import math

import jax
import jax.numpy as jnp
from jax import lax
from jax.experimental import pallas as pl
from jax.experimental.pallas import tpu as pltpu
from jax.sharding import PartitionSpec as P

HALO = 128
TAU = 0.05
ALPHA = 0.95
BLOCK = 256
LANES = 128
MESH = pl.DeviceIdType.MESH


def soft(diff):
    return diff * lax.rsqrt(diff * diff + TAU * TAU)


def gelu(x):
    return 0.5 * x * (1.0 + jnp.tanh(math.sqrt(2.0 / math.pi) * (x + 0.044715 * (x * x * x))))


def kernel(
    members,
    spaces,
    x_hbm,
    gain_ref,
    ws_hbm,
    wn_hbm,
    wo_hbm,
    readout_ref,
    edge_ref,
    truth_ref,
    var_ref,
    area_ref,
    grads_out,
    decoder_out,
    x_ref,
    ws_ref,
    wn_ref,
    wo_ref,
    ext_ref,
    hidden_ref,
    wide_ref,
    read_ref,
    truth_t,
    var_pad,
    f_ref,
    fr_ref,
    gs_ref,
    g_ref,
    d_ref,
    ds_ref,
    dr_ref,
    z_ref,
    ag_ref,
    load_sem,
    halo_send,
    halo_recv,
    f_send,
    f_recv,
    g_send,
    g_recv,
    d_send,
    d_recv,
    z_send,
    z_recv,
    ag_send,
    ag_recv,
):
    me = lax.axis_index("member")
    sp = lax.axis_index("space")
    nodes, width = x_ref.shape
    variables = readout_ref.shape[0]
    blocks = nodes // BLOCK
    part = BLOCK // members
    rows = width // members

    def load(src, dst, sem):
        return pltpu.make_async_copy(src, dst, load_sem.at[sem])

    x_parts = ((0, HALO), (nodes - HALO, HALO), (HALO, nodes - 2 * HALO))
    loads = [load(x_hbm.at[pl.ds(a, n)], x_ref.at[pl.ds(a, n)], i) for i, (a, n) in enumerate(x_parts)]
    loads += [load(ws_hbm, ws_ref, 3), load(wn_hbm, wn_ref, 4), load(wo_hbm, wo_ref, 5)]
    for item in loads:
        item.start()

    barrier = pltpu.get_barrier_semaphore()
    for d in range(1, members):
        pl.semaphore_signal(barrier, inc=1, device_id={"member": lax.rem(me + d, members)}, device_id_type=MESH)
    for d in range(1, spaces):
        pl.semaphore_signal(barrier, inc=1, device_id={"space": lax.rem(sp + d, spaces)}, device_id_type=MESH)

    gain = gain_ref[...].astype(jnp.float32)

    def norm(start, count):
        values = x_ref[pl.ds(start, count), :].astype(jnp.float32)
        scale = lax.rsqrt(jnp.mean(values * values, axis=-1, keepdims=True) + 1e-06)
        ext_ref[pl.ds(start + HALO, count), :] = (values * scale * gain).astype(jnp.bfloat16)

    loads[0].wait()
    norm(0, HALO)
    loads[1].wait()
    norm(nodes - HALO, HALO)

    pl.semaphore_wait(barrier, members - 1 + spaces - 1)

    down = pltpu.make_async_remote_copy(
        src_ref=ext_ref.at[pl.ds(HALO, HALO)],
        dst_ref=ext_ref.at[pl.ds(nodes + HALO, HALO)],
        send_sem=halo_send.at[0],
        recv_sem=halo_recv.at[0],
        device_id={"space": jnp.maximum(sp - 1, 0)},
        device_id_type=MESH,
    )
    up = pltpu.make_async_remote_copy(
        src_ref=ext_ref.at[pl.ds(nodes, HALO)],
        dst_ref=ext_ref.at[pl.ds(0, HALO)],
        send_sem=halo_send.at[1],
        recv_sem=halo_recv.at[1],
        device_id={"space": jnp.minimum(sp + 1, spaces - 1)},
        device_id_type=MESH,
    )

    @pl.when(sp > 0)
    def _():
        down.start()

    @pl.when(sp < spaces - 1)
    def _():
        up.start()

    @pl.when(sp == 0)
    def _():
        ext_ref[pl.ds(0, HALO), :] = jnp.zeros((HALO, width), jnp.bfloat16)

    @pl.when(sp == spaces - 1)
    def _():
        ext_ref[pl.ds(nodes + HALO, HALO), :] = jnp.zeros((HALO, width), jnp.bfloat16)

    loads[2].wait()
    lax.fori_loop(1, nodes // HALO - 1, lambda i, _: (norm(pl.multiple_of(i * HALO, HALO), HALO), 0)[1], 0)

    wide_ref[...] = jnp.zeros_like(wide_ref)
    wide_ref[pl.ds(0, variables), :] = readout_ref[...].astype(jnp.float32)
    read_ref[...] = wide_ref[...].astype(jnp.bfloat16)
    wide2 = d_ref
    wide2[...] = jnp.zeros_like(wide2)
    wide2[pl.ds(0, variables), pl.ds(0, nodes)] = truth_ref[...]
    wide2[pl.ds(variables, 1), pl.ds(0, nodes)] = area_ref[...]
    for j in range(nodes // LANES):
        at = j * LANES
        tile = wide2[:, pl.ds(at, LANES)].T
        per = LANES // part
        block, owner = at // BLOCK, (at % BLOCK) // part
        for k in range(per):
            truth_t[block, owner + k] = tile[k * part : (k + 1) * part, :]
    var_pad[...] = jnp.zeros_like(var_pad)
    var_pad[pl.ds(0, 1), pl.ds(0, variables)] = var_ref[...]
    d_ref[...] = jnp.zeros_like(d_ref)

    for item in loads[3:]:
        item.wait()

    def f_copy(b, d):
        return pltpu.make_async_remote_copy(
            src_ref=f_ref.at[b, lax.rem(me + d, members)],
            dst_ref=fr_ref.at[b, d],
            send_sem=f_send.at[b, d],
            recv_sem=f_recv.at[b, d],
            device_id={"member": lax.rem(me + d, members)},
            device_id_type=MESH,
        )

    def g_copy(b, d):
        return pltpu.make_async_remote_copy(
            src_ref=gs_ref.at[b, d],
            dst_ref=g_ref.at[b, me],
            send_sem=g_send.at[b, d],
            recv_sem=g_recv.at[b, d],
            device_id={"member": lax.rem(me + members - d, members)},
            device_id_type=MESH,
        )

    def advance(b):
        start = pl.multiple_of(b * BLOCK, BLOCK)
        local = edge_ref[pl.ds(start, BLOCK), :] - start
        columns = lax.broadcasted_iota(jnp.int32, (BLOCK, BLOCK + 2 * HALO), 1)
        count = jnp.zeros((BLOCK, BLOCK + 2 * HALO), jnp.float32)
        for k in range(edge_ref.shape[1]):
            count = count + jnp.where(local[:, k : k + 1] == columns, 1.0, 0.0)
        near = ext_ref[pl.ds(start, BLOCK + 2 * HALO), :]
        mean = jnp.dot(count.astype(jnp.bfloat16), near, preferred_element_type=jnp.float32)
        mean = (mean * (1.0 / edge_ref.shape[1])).astype(jnp.bfloat16)
        own = ext_ref[pl.ds(start + HALO, BLOCK), :]
        inside = jnp.dot(own, ws_ref[...], preferred_element_type=jnp.float32) + jnp.dot(
            mean, wn_ref[...], preferred_element_type=jnp.float32
        )
        activated = gelu(inside).astype(jnp.bfloat16)
        update = jnp.dot(activated, wo_ref[...], preferred_element_type=jnp.float32)
        hidden = (x_ref[pl.ds(start, BLOCK), :].astype(jnp.float32) + update).astype(jnp.bfloat16)
        hidden_ref[pl.ds(start, BLOCK), :] = hidden
        forecast = lax.dot_general(
            hidden, read_ref[...], (((1,), (1,)), ((), ())), preferred_element_type=jnp.float32
        )
        f_ref[b] = forecast.reshape(members, part, LANES)
        for d in range(1, members):
            f_copy(b, d).start()

    eps = (1.0 - ALPHA) / members
    couple = (1.0 - eps) / (members - 1)

    def score(b):
        for d in range(1, members):
            f_copy(b, d).wait_recv()
        truth = truth_t[b, me]
        weight = var_pad[pl.ds(0, 1), :] * truth[:, variables : variables + 1]
        values = [f_ref[b, me]] + [fr_ref[b, d] for d in range(1, members)]
        spread = [jnp.zeros((part, LANES), jnp.float32) for _ in range(members)]
        for i in range(members):
            for j in range(i + 1, members):
                sign = soft(values[i] - values[j])
                spread[i] = spread[i] + sign
                spread[j] = spread[j] - sign
        for d in range(members):
            grad = (weight * (soft(values[d] - truth) - couple * spread[d])).astype(jnp.bfloat16)
            if d == 0:
                g_ref[b, me] = grad
            else:
                gs_ref[b, d] = grad
                g_copy(b, d).start()

    def collect(b):
        start = pl.multiple_of(b * BLOCK, BLOCK)
        for d in range(1, members):
            g_copy(b, d).wait_recv()
        grads = g_ref[b].reshape(BLOCK, LANES)
        grads_out[pl.ds(start, BLOCK), :] = grads
        d_ref[...] += lax.dot_general(
            grads,
            hidden_ref[pl.ds(start, BLOCK), :],
            (((0,), (0,)), ((), ())),
            preferred_element_type=jnp.float32,
        )

    def order(i):
        return lax.rem(i + 1, blocks)

    def step(i, carry):
        @pl.when(i == blocks - 2)
        def _():
            @pl.when(sp > 0)
            def _():
                up.wait_recv()

            @pl.when(sp < spaces - 1)
            def _():
                down.wait_recv()

        advance(order(i))

        @pl.when(i >= 1)
        def _():
            score(order(i - 1))

        @pl.when(i >= 2)
        def _():
            collect(order(i - 2))

        return carry

    lax.fori_loop(0, blocks, step, 0)
    score(order(blocks - 1))
    collect(order(blocks - 2))
    collect(order(blocks - 1))

    ds_ref[...] = d_ref[...].T.reshape(members, rows, LANES).astype(jnp.bfloat16)

    def d_copy(d):
        return pltpu.make_async_remote_copy(
            src_ref=ds_ref.at[lax.rem(me + d, members)],
            dst_ref=dr_ref.at[d],
            send_sem=d_send.at[d],
            recv_sem=d_recv.at[d],
            device_id={"member": lax.rem(me + d, members)},
            device_id_type=MESH,
        )

    def z_copy(d):
        return pltpu.make_async_remote_copy(
            src_ref=z_ref.at[sp],
            dst_ref=z_ref.at[sp],
            send_sem=z_send.at[d],
            recv_sem=z_recv.at[d],
            device_id={"space": lax.rem(sp + d, spaces)},
            device_id_type=MESH,
        )

    def ag_copy(d):
        return pltpu.make_async_remote_copy(
            src_ref=ag_ref.at[me],
            dst_ref=ag_ref.at[me],
            send_sem=ag_send.at[d],
            recv_sem=ag_recv.at[d],
            device_id={"member": lax.rem(me + d, members)},
            device_id_type=MESH,
        )

    for d in range(1, members):
        d_copy(d).start()
    total = ds_ref[me].astype(jnp.float32)
    for d in range(1, members):
        d_copy(d).wait_recv()
        total = total + dr_ref[d].astype(jnp.float32)
    z_ref[sp] = total.astype(jnp.bfloat16)
    for d in range(1, spaces):
        z_copy(d).start()
    for d in range(1, spaces):
        z_copy(d).wait_recv()
    total = z_ref[0].astype(jnp.float32)
    for s in range(1, spaces):
        total = total + z_ref[s].astype(jnp.float32)
    ag_ref[me] = (total / math.sqrt(members * nodes * spaces)).astype(jnp.bfloat16)
    for d in range(1, members):
        ag_copy(d).start()
    for d in range(1, members):
        ag_copy(d).wait_recv()
    decoder_out[...] = ag_ref[...].reshape(width, LANES)

    @pl.when(sp > 0)
    def _():
        down.wait_send()

    @pl.when(sp < spaces - 1)
    def _():
        up.wait_send()

    def drain(b, carry):
        for d in range(1, members):
            f_copy(b, d).wait_send()
            g_copy(b, d).wait_send()
        return carry

    lax.fori_loop(0, blocks, drain, 0)
    for d in range(1, members):
        d_copy(d).wait_send()
        ag_copy(d).wait_send()
    for d in range(1, spaces):
        z_copy(d).wait_send()


def local(
    realization_channels,
    node_gain,
    w_self,
    w_neighbour,
    w_out,
    readout_map,
    edge_index,
    verifying_truth,
    var_weight,
    area_weight,
):
    members, spaces = lax.axis_size("member"), lax.axis_size("space")
    x = realization_channels[0]
    nodes, width = x.shape
    variables = readout_map.shape[0]
    blocks, part, rows = nodes // BLOCK, BLOCK // members, width // members
    bf16, f32 = jnp.bfloat16, jnp.float32
    dma = pltpu.SemaphoreType.DMA
    hbm, vmem = pl.BlockSpec(memory_space=pl.ANY), pl.BlockSpec(memory_space=pltpu.VMEM)
    grads, decoder = pl.pallas_call(
        functools.partial(kernel, members, spaces),
        out_shape=(
            jax.ShapeDtypeStruct((nodes, LANES), bf16),
            jax.ShapeDtypeStruct((width, LANES), bf16),
        ),
        in_specs=[hbm, vmem, hbm, hbm, hbm, vmem, vmem, vmem, vmem, vmem],
        out_specs=(vmem, vmem),
        scratch_shapes=[
            pltpu.VMEM((nodes, width), bf16),
            pltpu.VMEM((width, width), bf16),
            pltpu.VMEM((width, width), bf16),
            pltpu.VMEM((width, width), bf16),
            pltpu.VMEM((nodes + 2 * HALO, width), bf16),
            pltpu.VMEM((nodes, width), bf16),
            pltpu.VMEM((LANES, width), f32),
            pltpu.VMEM((LANES, width), bf16),
            pltpu.VMEM((blocks, members, part, LANES), f32),
            pltpu.VMEM((8, LANES), f32),
            pltpu.VMEM((blocks, members, part, LANES), f32),
            pltpu.VMEM((blocks, members, part, LANES), f32),
            pltpu.VMEM((blocks, members, part, LANES), bf16),
            pltpu.VMEM((blocks, members, part, LANES), bf16),
            pltpu.VMEM((LANES, max(width, nodes)), f32),
            pltpu.VMEM((members, rows, LANES), bf16),
            pltpu.VMEM((members, rows, LANES), bf16),
            pltpu.VMEM((spaces, rows, LANES), bf16),
            pltpu.VMEM((members, rows, LANES), bf16),
            dma((6,)),
            dma((2,)),
            dma((2,)),
            dma((blocks, members)),
            dma((blocks, members)),
            dma((blocks, members)),
            dma((blocks, members)),
            dma((members,)),
            dma((members,)),
            dma((spaces,)),
            dma((spaces,)),
            dma((members,)),
            dma((members,)),
        ],
        compiler_params=pltpu.CompilerParams(
            collective_id=0, has_side_effects=True, vmem_limit_bytes=48 * 2**20
        ),
    )(
        x,
        node_gain[None],
        w_self,
        w_neighbour,
        w_out,
        readout_map,
        edge_index,
        verifying_truth,
        var_weight[None],
        area_weight[None],
    )
    grad_hidden = jnp.dot(grads[:, :variables], readout_map, preferred_element_type=f32).astype(bf16)
    grad_decoder = decoder[:, :variables].T.astype(f32)
    return grad_hidden[None], grad_decoder


def solution(mesh):
    return jax.shard_map(
        local,
        mesh=mesh,
        in_specs=(
            P("member", "space", None),
            P(),
            P(),
            P(),
            P(),
            P(),
            P("space", None),
            P(None, "space"),
            P(),
            P("space"),
        ),
        out_specs=(P("member", "space", None), P()),
        check_vma=False,
    )
```

```python
import functools
import math

import jax
import jax.numpy as jnp
from jax import lax
from jax.experimental import pallas as pl
from jax.experimental.pallas import tpu as pltpu
from jax.sharding import PartitionSpec as P

HALO = 128
TAU = 0.05
ALPHA = 0.95
BLOCK = 256
LANES = 128
MESH = pl.DeviceIdType.MESH


def soft(diff):
    return diff * lax.rsqrt(diff * diff + TAU * TAU)


def gelu(x):
    return 0.5 * x * (1.0 + jnp.tanh(math.sqrt(2.0 / math.pi) * (x + 0.044715 * (x * x * x))))


def kernel(
    members,
    spaces,
    x_hbm,
    gain_hbm,
    ws_hbm,
    wn_hbm,
    wo_hbm,
    readout_hbm,
    edge_hbm,
    truth_hbm,
    var_hbm,
    area_hbm,
    grads_out,
    decoder_out,
    x_ref,
    gain_ref,
    readout_ref,
    edge_rows,
    edge_ref,
    truth_ref,
    var_ref,
    area_ref,
    ws_ref,
    wn_ref,
    wo_ref,
    ext_ref,
    hidden_ref,
    wide_ref,
    read_ref,
    truth_t,
    var_pad,
    f_ref,
    fr_ref,
    gs_ref,
    g_ref,
    d_ref,
    ds_ref,
    dr_ref,
    z_ref,
    ag_ref,
    load_sem,
    halo_send,
    halo_recv,
    f_send,
    f_recv,
    g_send,
    g_recv,
    d_send,
    d_recv,
    z_send,
    z_recv,
    ag_send,
    ag_recv,
):
    me = lax.axis_index("member")
    sp = lax.axis_index("space")
    nodes, width = x_ref.shape
    variables = readout_ref.shape[0]
    blocks = nodes // BLOCK
    part = BLOCK // members
    rows = width // members

    def load(src, dst, sem):
        return pltpu.make_async_copy(src, dst, load_sem.at[sem])

    x_parts = ((0, HALO), (nodes - HALO, HALO), (HALO, nodes - 2 * HALO))
    loads = [load(x_hbm.at[pl.ds(a, n)], x_ref.at[pl.ds(a, n)], i) for i, (a, n) in enumerate(x_parts)]
    loads += [load(ws_hbm, ws_ref, 3), load(wn_hbm, wn_ref, 4), load(wo_hbm, wo_ref, 5)]
    small = [
        load(gain_hbm, gain_ref, 6),
        load(edge_hbm, edge_rows, 7),
        load(readout_hbm, readout_ref, 8),
        load(truth_hbm, truth_ref, 9),
        load(var_hbm, var_ref, 10),
        load(area_hbm, area_ref, 11),
    ]
    for item in small[:1] + loads[:3] + small[1:] + loads[3:]:
        item.start()

    barrier = pltpu.get_barrier_semaphore()
    for d in range(1, members):
        pl.semaphore_signal(barrier, inc=1, device_id={"member": lax.rem(me + d, members)}, device_id_type=MESH)
    for d in range(1, spaces):
        pl.semaphore_signal(barrier, inc=1, device_id={"space": lax.rem(sp + d, spaces)}, device_id_type=MESH)

    small[0].wait()
    gain = gain_ref[...].astype(jnp.float32)[None, :]

    def norm(start, count):
        values = x_ref[pl.ds(start, count), :].astype(jnp.float32)
        scale = lax.rsqrt(jnp.mean(values * values, axis=-1, keepdims=True) + 1e-06)
        ext_ref[pl.ds(start + HALO, count), :] = (values * scale * gain).astype(jnp.bfloat16)

    loads[0].wait()
    norm(0, HALO)
    loads[1].wait()
    norm(nodes - HALO, HALO)

    pl.semaphore_wait(barrier, members - 1 + spaces - 1)

    down = pltpu.make_async_remote_copy(
        src_ref=ext_ref.at[pl.ds(HALO, HALO)],
        dst_ref=ext_ref.at[pl.ds(nodes + HALO, HALO)],
        send_sem=halo_send.at[0],
        recv_sem=halo_recv.at[0],
        device_id={"space": jnp.maximum(sp - 1, 0)},
        device_id_type=MESH,
    )
    up = pltpu.make_async_remote_copy(
        src_ref=ext_ref.at[pl.ds(nodes, HALO)],
        dst_ref=ext_ref.at[pl.ds(0, HALO)],
        send_sem=halo_send.at[1],
        recv_sem=halo_recv.at[1],
        device_id={"space": jnp.minimum(sp + 1, spaces - 1)},
        device_id_type=MESH,
    )

    @pl.when(sp > 0)
    def _():
        down.start()

    @pl.when(sp < spaces - 1)
    def _():
        up.start()

    @pl.when(sp == 0)
    def _():
        ext_ref[pl.ds(0, HALO), :] = jnp.zeros((HALO, width), jnp.bfloat16)

    @pl.when(sp == spaces - 1)
    def _():
        ext_ref[pl.ds(nodes + HALO, HALO), :] = jnp.zeros((HALO, width), jnp.bfloat16)

    loads[2].wait()
    lax.fori_loop(1, nodes // HALO - 1, lambda i, _: (norm(pl.multiple_of(i * HALO, HALO), HALO), 0)[1], 0)

    for item in small[1:]:
        item.wait()
    edge_ref[...] = edge_rows[...].T
    wide_ref[...] = jnp.zeros_like(wide_ref)
    wide_ref[pl.ds(0, variables), :] = readout_ref[...].astype(jnp.float32)
    read_ref[...] = wide_ref[...].astype(jnp.bfloat16)
    wide2 = d_ref
    wide2[...] = jnp.zeros_like(wide2)
    wide2[pl.ds(0, variables), pl.ds(0, nodes)] = truth_ref[...]
    wide2[pl.ds(variables, 1), pl.ds(0, nodes)] = area_ref[...][None, :]
    for j in range(nodes // LANES):
        at = j * LANES
        tile = wide2[:, pl.ds(at, LANES)].T
        per = LANES // part
        block, owner = at // BLOCK, (at % BLOCK) // part
        for k in range(per):
            truth_t[block, owner + k] = tile[k * part : (k + 1) * part, :]
    var_pad[...] = jnp.zeros_like(var_pad)
    var_pad[pl.ds(0, 1), pl.ds(0, variables)] = var_ref[...][None, :]
    d_ref[...] = jnp.zeros_like(d_ref)

    for item in loads[3:]:
        item.wait()

    def f_copy(b, d):
        return pltpu.make_async_remote_copy(
            src_ref=f_ref.at[b, lax.rem(me + d, members)],
            dst_ref=fr_ref.at[b, d],
            send_sem=f_send.at[b, d],
            recv_sem=f_recv.at[b, d],
            device_id={"member": lax.rem(me + d, members)},
            device_id_type=MESH,
        )

    def g_copy(b, d):
        return pltpu.make_async_remote_copy(
            src_ref=gs_ref.at[b, d],
            dst_ref=g_ref.at[b, me],
            send_sem=g_send.at[b, d],
            recv_sem=g_recv.at[b, d],
            device_id={"member": lax.rem(me + members - d, members)},
            device_id_type=MESH,
        )

    def advance(b):
        start = pl.multiple_of(b * BLOCK, BLOCK)
        local = edge_ref[pl.ds(start, BLOCK), :] - start
        columns = lax.broadcasted_iota(jnp.int32, (BLOCK, BLOCK + 2 * HALO), 1)
        count = jnp.zeros((BLOCK, BLOCK + 2 * HALO), jnp.float32)
        for k in range(edge_ref.shape[1]):
            count = count + jnp.where(local[:, k : k + 1] == columns, 1.0, 0.0)
        near = ext_ref[pl.ds(start, BLOCK + 2 * HALO), :]
        mean = jnp.dot(count.astype(jnp.bfloat16), near, preferred_element_type=jnp.float32)
        mean = (mean * (1.0 / edge_ref.shape[1])).astype(jnp.bfloat16)
        own = ext_ref[pl.ds(start + HALO, BLOCK), :]
        inside = jnp.dot(own, ws_ref[...], preferred_element_type=jnp.float32) + jnp.dot(
            mean, wn_ref[...], preferred_element_type=jnp.float32
        )
        activated = gelu(inside).astype(jnp.bfloat16)
        update = jnp.dot(activated, wo_ref[...], preferred_element_type=jnp.float32)
        hidden = (x_ref[pl.ds(start, BLOCK), :].astype(jnp.float32) + update).astype(jnp.bfloat16)
        hidden_ref[pl.ds(start, BLOCK), :] = hidden
        forecast = lax.dot_general(
            hidden, read_ref[...], (((1,), (1,)), ((), ())), preferred_element_type=jnp.float32
        )
        f_ref[b] = forecast.reshape(members, part, LANES)
        for d in range(1, members):
            f_copy(b, d).start()

    eps = (1.0 - ALPHA) / members
    couple = (1.0 - eps) / (members - 1)

    def score(b):
        for d in range(1, members):
            f_copy(b, d).wait_recv()
        truth = truth_t[b, me]
        weight = var_pad[pl.ds(0, 1), :] * truth[:, variables : variables + 1]
        values = [f_ref[b, me]] + [fr_ref[b, d] for d in range(1, members)]
        spread = [jnp.zeros((part, LANES), jnp.float32) for _ in range(members)]
        for i in range(members):
            for j in range(i + 1, members):
                sign = soft(values[i] - values[j])
                spread[i] = spread[i] + sign
                spread[j] = spread[j] - sign
        for d in range(members):
            grad = (weight * (soft(values[d] - truth) - couple * spread[d])).astype(jnp.bfloat16)
            if d == 0:
                g_ref[b, me] = grad
            else:
                gs_ref[b, d] = grad
                g_copy(b, d).start()

    def collect(b):
        start = pl.multiple_of(b * BLOCK, BLOCK)
        for d in range(1, members):
            g_copy(b, d).wait_recv()
        grads = g_ref[b].reshape(BLOCK, LANES)
        grads_out[pl.ds(start, BLOCK), :] = grads
        d_ref[...] += lax.dot_general(
            grads,
            hidden_ref[pl.ds(start, BLOCK), :],
            (((0,), (0,)), ((), ())),
            preferred_element_type=jnp.float32,
        )

    def order(i):
        return lax.rem(i + 1, blocks)

    def step(i, carry):
        @pl.when(i == blocks - 2)
        def _():
            @pl.when(sp > 0)
            def _():
                up.wait_recv()

            @pl.when(sp < spaces - 1)
            def _():
                down.wait_recv()

        advance(order(i))

        @pl.when(i >= 1)
        def _():
            score(order(i - 1))

        @pl.when(i >= 2)
        def _():
            collect(order(i - 2))

        return carry

    lax.fori_loop(0, blocks, step, 0)
    score(order(blocks - 1))
    collect(order(blocks - 2))
    collect(order(blocks - 1))

    ds_ref[...] = d_ref[...].T.reshape(members, rows, LANES).astype(jnp.bfloat16)

    def d_copy(d):
        return pltpu.make_async_remote_copy(
            src_ref=ds_ref.at[lax.rem(me + d, members)],
            dst_ref=dr_ref.at[d],
            send_sem=d_send.at[d],
            recv_sem=d_recv.at[d],
            device_id={"member": lax.rem(me + d, members)},
            device_id_type=MESH,
        )

    def z_copy(d):
        return pltpu.make_async_remote_copy(
            src_ref=z_ref.at[sp],
            dst_ref=z_ref.at[sp],
            send_sem=z_send.at[d],
            recv_sem=z_recv.at[d],
            device_id={"space": lax.rem(sp + d, spaces)},
            device_id_type=MESH,
        )

    def ag_copy(d):
        return pltpu.make_async_remote_copy(
            src_ref=ag_ref.at[me],
            dst_ref=ag_ref.at[me],
            send_sem=ag_send.at[d],
            recv_sem=ag_recv.at[d],
            device_id={"member": lax.rem(me + d, members)},
            device_id_type=MESH,
        )

    for d in range(1, members):
        d_copy(d).start()
    total = ds_ref[me].astype(jnp.float32)
    for d in range(1, members):
        d_copy(d).wait_recv()
        total = total + dr_ref[d].astype(jnp.float32)
    z_ref[sp] = total.astype(jnp.bfloat16)
    for d in range(1, spaces):
        z_copy(d).start()
    for d in range(1, spaces):
        z_copy(d).wait_recv()
    total = z_ref[0].astype(jnp.float32)
    for s in range(1, spaces):
        total = total + z_ref[s].astype(jnp.float32)
    ag_ref[me] = (total / math.sqrt(members * nodes * spaces)).astype(jnp.bfloat16)
    for d in range(1, members):
        ag_copy(d).start()
    for d in range(1, members):
        ag_copy(d).wait_recv()
    decoder_out[...] = ag_ref[...].reshape(width, LANES)

    @pl.when(sp > 0)
    def _():
        down.wait_send()

    @pl.when(sp < spaces - 1)
    def _():
        up.wait_send()

    def drain(b, carry):
        for d in range(1, members):
            f_copy(b, d).wait_send()
            g_copy(b, d).wait_send()
        return carry

    lax.fori_loop(0, blocks, drain, 0)
    for d in range(1, members):
        d_copy(d).wait_send()
        ag_copy(d).wait_send()
    for d in range(1, spaces):
        z_copy(d).wait_send()


def local(
    realization_channels,
    node_gain,
    w_self,
    w_neighbour,
    w_out,
    readout_map,
    edge_index,
    verifying_truth,
    var_weight,
    area_weight,
):
    members, spaces = lax.axis_size("member"), lax.axis_size("space")
    x = realization_channels[0]
    nodes, width = x.shape
    variables = readout_map.shape[0]
    blocks, part, rows = nodes // BLOCK, BLOCK // members, width // members
    bf16, f32 = jnp.bfloat16, jnp.float32
    dma = pltpu.SemaphoreType.DMA
    hbm, vmem = pl.BlockSpec(memory_space=pltpu.HBM), pl.BlockSpec(memory_space=pltpu.VMEM)
    grads, decoder = pl.pallas_call(
        functools.partial(kernel, members, spaces),
        out_shape=(
            pltpu.VMEM((nodes, LANES), bf16),
            pltpu.VMEM((width, LANES), bf16),
        ),
        in_specs=[hbm] * 10,
        out_specs=(vmem, vmem),
        scratch_shapes=[
            pltpu.VMEM((nodes, width), bf16),
            pltpu.VMEM((width,), bf16),
            pltpu.VMEM((variables, width), bf16),
            pltpu.VMEM(edge_index.shape[::-1], jnp.int32),
            pltpu.VMEM(edge_index.shape, jnp.int32),
            pltpu.VMEM((variables, nodes), f32),
            pltpu.VMEM((variables,), f32),
            pltpu.VMEM((nodes,), f32),
            pltpu.VMEM((width, width), bf16),
            pltpu.VMEM((width, width), bf16),
            pltpu.VMEM((width, width), bf16),
            pltpu.VMEM((nodes + 2 * HALO, width), bf16),
            pltpu.VMEM((nodes, width), bf16),
            pltpu.VMEM((LANES, width), f32),
            pltpu.VMEM((LANES, width), bf16),
            pltpu.VMEM((blocks, members, part, LANES), f32),
            pltpu.VMEM((8, LANES), f32),
            pltpu.VMEM((blocks, members, part, LANES), f32),
            pltpu.VMEM((blocks, members, part, LANES), f32),
            pltpu.VMEM((blocks, members, part, LANES), bf16),
            pltpu.VMEM((blocks, members, part, LANES), bf16),
            pltpu.VMEM((LANES, max(width, nodes)), f32),
            pltpu.VMEM((members, rows, LANES), bf16),
            pltpu.VMEM((members, rows, LANES), bf16),
            pltpu.VMEM((spaces, rows, LANES), bf16),
            pltpu.VMEM((members, rows, LANES), bf16),
            dma((12,)),
            dma((2,)),
            dma((2,)),
            dma((blocks, members)),
            dma((blocks, members)),
            dma((blocks, members)),
            dma((blocks, members)),
            dma((members,)),
            dma((members,)),
            dma((spaces,)),
            dma((spaces,)),
            dma((members,)),
            dma((members,)),
        ],
        compiler_params=pltpu.CompilerParams(
            collective_id=0, has_side_effects=True, vmem_limit_bytes=61 * 2**20
        ),
    )(
        x,
        node_gain,
        w_self,
        w_neighbour,
        w_out,
        readout_map,
        edge_index.T,
        verifying_truth,
        var_weight,
        area_weight,
    )
    grad_hidden = jnp.dot(grads[:, :variables], readout_map, preferred_element_type=f32).astype(bf16)
    grad_decoder = decoder[:, :variables].T.astype(f32)
    return grad_hidden[None], grad_decoder


def solution(mesh):
    return jax.shard_map(
        local,
        mesh=mesh,
        in_specs=(
            P("member", "space", None),
            P(),
            P(),
            P(),
            P(),
            P(),
            P("space", None),
            P(None, "space"),
            P(),
            P("space"),
        ),
        out_specs=(P("member", "space", None), P()),
        check_vma=False,
    )
```
